32 devices in a mesh: segment: 2 (over core), et: 16 (over z, y, x).
Axes of the slice: x: 2, y: 2, z: 4, core: 2. Of those that a mesh axis runs over, the one named last changes fastest.
Arguments:
- inputs: bfloat16 [1, 16, 6144], P(None, 'et'), may hold values from -6 to 6
- cotangent: bfloat16 [1, 16, 6144], P(None, 'et'), may hold values from -6 to 6
- gate_weight: bfloat16 [2, 6144, 16384], P('segment', None, 'et'), may hold values from -0.078125 to 0.078125
- up_weight: bfloat16 [2, 6144, 16384], P('segment', None, 'et'), may hold values from -0.078125 to 0.078125
- down_weight: bfloat16 [2, 16384, 6144], P('segment', 'et'), may hold values from -0.0625 to 0.0625
- route_rows: int32 [2, 1, 16], P('segment'), may hold values from 0 to 15, as said below
- route_count: int32 [2, 1], P('segment'), may hold values from 4 to 16, as said below
- route_weight: float32 [2, 1, 16], P('segment'), may hold values from 0.05 to 1
- width_mask: int32 [2, 128], P('segment', 'et'), may hold values from 0 to 1, as said below
Outputs:
- section_output: bfloat16 [2, 1, 16, 6144], P('segment', None, 'et')
- grad_input: bfloat16 [2, 1, 16, 6144], P('segment', None, 'et')
- grad_gate: bfloat16 [2, 6144, 16384], P('segment', None, 'et')
- grad_up: bfloat16 [2, 6144, 16384], P('segment', None, 'et')
- grad_down: bfloat16 [2, 16384, 6144], P('segment', 'et')
The draws below stay inside these ranges and needn't reach their ends.
Inputs may be any that keep to these rules, and one draw needn't show every extreme that they name: `route_rows`: each list names every one of the 16 tokens once; its first route_count entries are the slots routed to the expert. `route_count`: 16 in at least one entry. `width_mask`: the kept tiles of each section are its first ones, at least 32 of them and never all.
All inputs are finite; a program needn't handle non-finite values.
Results may differ from the reference program's by a relative error of at most 0.015.
Values may be sent and summed in bfloat16 or wider, within the bound.
A program may use at most 256 MiB of HBM per device.

```python
import math
import jax
import jax.numpy as jnp
from jax import lax

D = 6144
FF = 16384
TILE = 128
MICRO = 1
SEGMENTS = 2
TOKENS = 16
SLOTS = 16
TILES = 128


def draw_route_rows(key, part):
    keys = jax.random.split(jax.random.fold_in(key, 11), SEGMENTS * MICRO)
    orders = jax.vmap(lambda single: jax.random.permutation(single, SLOTS))(keys)
    return orders.astype(jnp.int32).reshape(SEGMENTS, MICRO, SLOTS)


def draw_route_count(key, part):
    first_key = jax.random.fold_in(key, 21)
    second_key = jax.random.fold_in(key, 22)
    counts = jax.random.randint(first_key, (SEGMENTS * MICRO,), SLOTS // 4, SLOTS + 1).astype(jnp.int32)
    chosen = jax.random.randint(second_key, (), 0, SEGMENTS * MICRO).astype(jnp.int32)
    counts = counts.at[chosen].set(SLOTS)
    return counts.reshape(SEGMENTS, MICRO)


def draw_width_mask(key, part):
    widths = jax.random.randint(jax.random.fold_in(key, 31), (SEGMENTS, 1), TILES // 4, TILES).astype(jnp.int32)
    return (jnp.arange(TILES, dtype=jnp.int32)[None, :] < widths).astype(jnp.int32)


def steps_of(rng, shape, shards, low, top_value):
    loudness, own = 1.0, jax.random.fold_in(rng, 6)
    for dim, parts in shards:
        steps = jnp.exp(jax.random.uniform(jax.random.fold_in(own, dim), (parts,), jnp.float32, low / len(shards), top_value / len(shards)))
        loudness = loudness * jnp.repeat(steps, shape[dim] // parts).reshape([-1 if axis == dim else 1 for axis in range(len(shape))])
    return loudness


def gaussian(stream_key, extent, scale, reach, pieces=(), held_as=jnp.bfloat16):
    values = jax.random.normal(stream_key, extent, jnp.float32) * scale
    if len(pieces) > 0:
        values = steps_of(stream_key, extent, pieces, -0.22, 0.18) * values
    return jnp.clip(values, min=-reach, max=reach).astype(held_as)


def setup_inputs(seed: int = 0) -> dict:
    seeds = jax.random.split(jax.random.key(seed), 10)
    inputs = gaussian(seeds[0], (MICRO, TOKENS, D), 1.0, 6.0, ((1, 16),))
    cotangent = gaussian(seeds[1], (MICRO, TOKENS, D), 1.0, 6.0, ((1, 16),))
    gate_weight = gaussian(seeds[2], (SEGMENTS, D, FF), D ** -0.5, 0.078125, ((0, 2), (2, 16)))
    up_weight = gaussian(seeds[3], (SEGMENTS, D, FF), D ** -0.5, 0.078125, ((0, 2), (2, 16)))
    down_weight = gaussian(seeds[4], (SEGMENTS, FF, D), (FF // 2) ** -0.5, 0.0625, ((0, 2), (1, 16)))
    route_rows = draw_route_rows(jax.random.fold_in(seeds[9], 71), 0)
    route_count = draw_route_count(jax.random.fold_in(seeds[9], 71), 0)
    route_weight = jnp.clip(jnp.exp(math.log(1.0) - 2.9957323 * jax.random.uniform(seeds[7], (SEGMENTS, MICRO, SLOTS), jnp.float32) ** steps_of(seeds[7], (SEGMENTS, MICRO, SLOTS), ((0, 2),), -0.2, 0.2)), 0.05, 1.0)
    width_mask = draw_width_mask(jax.random.fold_in(seeds[9], 71), 0)
    return dict(inputs=inputs, cotangent=cotangent, gate_weight=gate_weight, up_weight=up_weight, down_weight=down_weight, route_rows=route_rows, route_count=route_count, route_weight=route_weight, width_mask=width_mask)


def expert_forward(picked, gate_w, up_w, down_w, keep):
    gate_value = jnp.dot(picked, gate_w, preferred_element_type=jnp.float32)
    up_value = jnp.dot(picked, up_w, preferred_element_type=jnp.float32)
    hidden = (gate_value * jax.nn.sigmoid(gate_value) * up_value * keep).astype(jnp.bfloat16)
    outcome = jnp.dot(hidden, down_w, preferred_element_type=jnp.float32)
    return gate_value, up_value, hidden, outcome


def expert_backward(picked, slot_grad_in, gate_value, up_value, hidden, gate_w, up_w, down_w, keep):
    contract_last = (((1,), (1,)), ((), ()))
    contract_first = (((0,), (0,)), ((), ()))
    hidden_delta = lax.dot_general(slot_grad_in, down_w, contract_last, preferred_element_type=jnp.float32)
    sig_gate = jax.nn.sigmoid(gate_value)
    gate_delta = (hidden_delta * keep * up_value * sig_gate * (1.0 + gate_value * (1.0 - sig_gate))).astype(jnp.bfloat16)
    up_delta = (hidden_delta * keep * gate_value * sig_gate).astype(jnp.bfloat16)
    grad_gate = lax.dot_general(picked, gate_delta, contract_first, preferred_element_type=jnp.float32)
    grad_up = lax.dot_general(picked, up_delta, contract_first, preferred_element_type=jnp.float32)
    grad_down = lax.dot_general(hidden, slot_grad_in, contract_first, preferred_element_type=jnp.float32)
    slot_grad = lax.dot_general(gate_delta, gate_w, contract_last, preferred_element_type=jnp.float32)
    slot_grad = slot_grad + lax.dot_general(up_delta, up_w, contract_last, preferred_element_type=jnp.float32)
    return grad_gate, grad_up, grad_down, slot_grad


def reference(inputs, cotangent, gate_weight, up_weight, down_weight, route_rows, route_count, route_weight, width_mask):
    slot_index = jnp.arange(SLOTS, dtype=jnp.int32)
    keeps = [jnp.repeat(width_mask[s].astype(jnp.float32), TILE) for s in range(SEGMENTS)]
    current = [inputs[m] for m in range(MICRO)]
    saved = []
    outputs = []
    for s in range(SEGMENTS):
        saved_segment = []
        results = []
        for m in range(MICRO):
            slot_rows = route_rows[s, m]
            scale = jnp.where(slot_index < route_count[s, m], route_weight[s, m], 0.0)
            picked = current[m][slot_rows]
            gate_value, up_value, hidden, outcome = expert_forward(picked, gate_weight[s], up_weight[s], down_weight[s], keeps[s])
            added = jnp.zeros((TOKENS, D), jnp.float32).at[slot_rows].add(scale[:, None] * outcome)
            results.append((current[m].astype(jnp.float32) + added).astype(jnp.bfloat16))
            saved_segment.append((picked, gate_value, up_value, hidden, scale))
        saved.append(saved_segment)
        outputs.append(jnp.stack(results))
        current = results
    upstream = [cotangent[m] for m in range(MICRO)]
    grad_inputs = [None] * SEGMENTS
    grads_gate = [None] * SEGMENTS
    grads_up = [None] * SEGMENTS
    grads_down = [None] * SEGMENTS
    for s in reversed(range(SEGMENTS)):
        acc_gate = jnp.zeros((D, FF), jnp.float32)
        acc_up = jnp.zeros((D, FF), jnp.float32)
        acc_down = jnp.zeros((FF, D), jnp.float32)
        results = []
        for m in range(MICRO):
            picked, gate_value, up_value, hidden, scale = saved[s][m]
            slot_rows = route_rows[s, m]
            slot_grad_in = (scale[:, None] * upstream[m][slot_rows].astype(jnp.float32)).astype(jnp.bfloat16)
            part_gate, part_up, part_down, slot_grad = expert_backward(picked, slot_grad_in, gate_value, up_value, hidden, gate_weight[s], up_weight[s], down_weight[s], keeps[s])
            acc_gate = acc_gate + part_gate
            acc_up = acc_up + part_up
            acc_down = acc_down + part_down
            added = jnp.zeros((TOKENS, D), jnp.float32).at[slot_rows].add(slot_grad)
            results.append((upstream[m].astype(jnp.float32) + added).astype(jnp.bfloat16))
        grad_inputs[s] = jnp.stack(results)
        grads_gate[s] = acc_gate.astype(jnp.bfloat16)
        grads_up[s] = acc_up.astype(jnp.bfloat16)
        grads_down[s] = acc_down.astype(jnp.bfloat16)
        upstream = results
    return (jnp.stack(outputs), jnp.stack(grad_inputs), jnp.stack(grads_gate), jnp.stack(grads_up), jnp.stack(grads_down))
```

```python
import functools
import jax
import jax.numpy as jnp
from jax import lax
from jax.experimental import pallas as pl
from jax.experimental.pallas import tpu as pltpu
from jax.sharding import PartitionSpec as P

MESH = pl.DeviceIdType.MESH
F32 = jnp.float32
BF16 = jnp.bfloat16
FOLD = 16
LAST = (((1,), (1,)), ((), ()))
FIRST = (((0,), (0,)), ((), ()))


def chunk_of(width):
    for size in (768, 512, 256, 128):
        if width % size == 0:
            return size
    return width


def chain_kernel(
    n,
    chunk,
    row_ref,
    scale_ref,
    keep_ref,
    gate_hbm,
    up_hbm,
    down_hbm,
    first_out,
    second_out,
    u_ref,
    sgi_ref,
    gd_ref,
    ud_ref,
    hid_ref,
    gate_w,
    up_w,
    down_w,
    first_all,
    second_all,
    send_a,
    send_b,
    recv_a,
    recv_b,
    fold_ref,
    part_ref,
    gate_val,
    up_val,
    load_sem,
    send_sem,
    recv_sem,
):
    seg = lax.axis_index("segment")
    me = lax.axis_index("et")
    other = 1 - seg
    width = u_ref.shape[1]
    hidden_cols = gate_w.shape[1]
    tokens = u_ref.shape[0]
    quota = width // FOLD
    steps = width // chunk

    def span(c):
        return pl.ds(pl.multiple_of(c * chunk, chunk), chunk)

    def load_gate(c):
        return pltpu.make_async_copy(gate_hbm.at[span(c)], gate_w.at[span(c)], load_sem.at[0, c])

    def load_up(c):
        return pltpu.make_async_copy(up_hbm.at[span(c)], up_w.at[span(c)], load_sem.at[1, c])

    def load_down(c):
        return pltpu.make_async_copy(
            down_hbm.at[:, span(c)], down_w.at[:, span(c)], load_sem.at[2, c]
        )

    @pl.when(seg == 0)
    def _():
        for c in range(steps):
            load_gate(c).start()
            load_up(c).start()
        for c in range(steps):
            load_down(c).start()

    @pl.when(seg == 1)
    def _():
        for c in range(steps):
            load_down(c).start()
        for c in range(steps):
            load_gate(c).start()
            load_up(c).start()

    barrier = pltpu.get_barrier_semaphore()

    def greet(k, _):
        pl.semaphore_signal(barrier, inc=1, device_id=(other, k), device_id_type=MESH)
        return 0

    def greet_own(k, _):
        pl.semaphore_signal(
            barrier, inc=1, device_id=(seg, lax.rem(me + k, n)), device_id_type=MESH
        )
        return 0

    lax.fori_loop(1, n, greet_own, 0)
    lax.fori_loop(0, n, greet, 0)
    pl.semaphore_wait(barrier, 2 * n - 1)

    def remote(src, dst, stage, to_seg, to_et):
        return pltpu.make_async_remote_copy(
            src_ref=src,
            dst_ref=dst,
            send_sem=send_sem.at[stage],
            recv_sem=recv_sem.at[stage],
            device_id=(to_seg, to_et),
            device_id_type=MESH,
        )

    def wait_bytes(buffer, count, sem):
        piece = buffer.at[pl.ds(0, count)]
        pltpu.make_async_copy(piece, piece, sem).wait()

    def send_first():
        def body(k, _):
            remote(row_ref, first_all.at[me], 0, seg, lax.rem(me + k, n)).start()
            return 0

        lax.fori_loop(1, n, body, 0)
        first_all[pl.ds(me, 1)] = row_ref[...][None]

    def send_second(src):
        def body(k, _):
            remote(src, second_all.at[me], 1, other, lax.rem(me + k, n)).start()
            return 0

        lax.fori_loop(0, n, body, 0)

    def unfold(buffer, out, scaled):
        fold_ref[...] = buffer[...].astype(F32)
        for j in range(FOLD):
            piece = fold_ref[:, j, :]
            if scaled:
                piece = piece * scale_ref[:, 0:1]
            out[:, j * quota : (j + 1) * quota] = piece.astype(BF16)

    def scatter(send, recv, stage):
        for j in range(FOLD):
            fold_ref[:, j, :] = part_ref[:, j * quota : (j + 1) * quota]
        send[...] = fold_ref[...].astype(BF16)

        def body(k, _):
            peer = lax.rem(me + k, n)
            remote(send.at[peer], recv.at[me], stage, seg, peer).start()
            return 0

        lax.fori_loop(1, n, body, 0)
        recv[pl.ds(me, 1)] = send[pl.ds(me, 1)]

    def gathered_sum(recv, stage):
        wait_bytes(recv, n - 1, recv_sem.at[stage])

        def body(k, total):
            return total + recv[k].astype(F32)

        return lax.fori_loop(0, n, body, jnp.zeros((FOLD, quota), F32))

    def project():
        def body(c, carry):
            gate_acc, up_acc = carry
            load_gate(c).wait()
            load_up(c).wait()
            rows = u_ref[:, span(c)]
            gate_acc = gate_acc + jnp.dot(rows, gate_w[span(c), :], preferred_element_type=F32)
            up_acc = up_acc + jnp.dot(rows, up_w[span(c), :], preferred_element_type=F32)
            return gate_acc, up_acc

        zero = jnp.zeros((tokens, hidden_cols), F32)
        gate_acc, up_acc = lax.fori_loop(0, steps, body, (zero, zero))
        gate_val[...] = gate_acc
        up_val[...] = up_acc
        hid_ref[...] = (gate_acc * jax.nn.sigmoid(gate_acc) * up_acc * keep_ref[...]).astype(BF16)

    def outcome(loads):
        def body(c, _):
            if loads:
                load_down(c).wait()
            value = jnp.dot(hid_ref[...], down_w[:, span(c)], preferred_element_type=F32)
            part_ref[:, span(c)] = value * scale_ref[:, 0:1]
            return 0

        lax.fori_loop(0, steps, body, 0)

    def hidden_delta(loads):
        def body(c, acc):
            if loads:
                load_down(c).wait()
            return acc + lax.dot_general(
                sgi_ref[:, span(c)], down_w[:, span(c)], LAST, preferred_element_type=F32
            )

        return lax.fori_loop(0, steps, body, jnp.zeros((tokens, hidden_cols), F32))

    def deltas(delta):
        gate_value = gate_val[...]
        sig = jax.nn.sigmoid(gate_value)
        kept = delta * keep_ref[...]
        gd_ref[...] = (kept * up_val[...] * sig * (1.0 + gate_value * (1.0 - sig))).astype(BF16)
        ud_ref[...] = (kept * gate_value * sig).astype(BF16)

    def slot_gradient():
        def body(c, _):
            value = lax.dot_general(
                gd_ref[...], gate_w[span(c), :], LAST, preferred_element_type=F32
            )
            part_ref[:, span(c)] = value + lax.dot_general(
                ud_ref[...], up_w[span(c), :], LAST, preferred_element_type=F32
            )
            return 0

        lax.fori_loop(0, steps, body, 0)

    send_first()

    @pl.when(seg == 0)
    def _():
        wait_bytes(first_all, n - 1, recv_sem.at[0])
        unfold(first_all, u_ref, False)
        project()
        outcome(True)
        scatter(send_a, recv_a, 2)
        total = gathered_sum(recv_a, 2)
        first_out[...] = (row_ref[...].astype(F32) + total).astype(BF16)
        send_second(first_out)
        wait_bytes(second_all, n, recv_sem.at[1])
        unfold(second_all, sgi_ref, True)
        deltas(hidden_delta(False))
        slot_gradient()
        scatter(send_b, recv_b, 3)
        total = gathered_sum(recv_b, 3)
        second_out[...] = (second_all[me].astype(F32) + total).astype(BF16)

    @pl.when(seg == 1)
    def _():
        wait_bytes(first_all, n - 1, recv_sem.at[0])
        unfold(first_all, sgi_ref, True)
        part_ref[:, 0:hidden_cols] = hidden_delta(True)
        wait_bytes(second_all, n, recv_sem.at[1])
        unfold(second_all, u_ref, False)
        project()
        deltas(part_ref[:, 0:hidden_cols])
        slot_gradient()
        scatter(send_a, recv_a, 2)
        total = gathered_sum(recv_a, 2)
        first_out[...] = (row_ref[...].astype(F32) + total).astype(BF16)
        send_second(first_out)
        outcome(False)
        scatter(send_b, recv_b, 3)
        total = gathered_sum(recv_b, 3)
        second_out[...] = (second_all[me].astype(F32) + total).astype(BF16)

    wait_bytes(first_all, n - 1, send_sem.at[0])
    wait_bytes(second_all, n, send_sem.at[1])
    wait_bytes(send_a, n - 1, send_sem.at[2])
    wait_bytes(send_b, n - 1, send_sem.at[3])


def chain(n, row, scale, keep, gate_w, up_w, down_w):
    tokens = scale.shape[0]
    width, hidden_cols = gate_w.shape
    quota = width // FOLD
    chunk = chunk_of(width)
    vmem = pl.BlockSpec(memory_space=pltpu.VMEM)
    hbm = pl.BlockSpec(memory_space=pl.ANY)
    shape = jax.ShapeDtypeStruct
    buffers = [pltpu.VMEM((n, FOLD, quota), BF16)] * 6
    return pl.pallas_call(
        functools.partial(chain_kernel, n, chunk),
        out_shape=(
            shape((FOLD, quota), BF16),
            shape((FOLD, quota), BF16),
            shape((tokens, width), BF16),
            shape((tokens, width), BF16),
            shape((tokens, hidden_cols), BF16),
            shape((tokens, hidden_cols), BF16),
            shape((tokens, hidden_cols), BF16),
        ),
        in_specs=[vmem, vmem, vmem, hbm, hbm, hbm],
        out_specs=(vmem,) * 7,
        scratch_shapes=[
            pltpu.VMEM((width, hidden_cols), BF16),
            pltpu.VMEM((width, hidden_cols), BF16),
            pltpu.VMEM((hidden_cols, width), BF16),
            *buffers,
            pltpu.VMEM((n, FOLD, quota), F32),
            pltpu.VMEM((tokens, width), F32),
            pltpu.VMEM((tokens, hidden_cols), F32),
            pltpu.VMEM((tokens, hidden_cols), F32),
            pltpu.SemaphoreType.DMA((3, width // chunk)),
            pltpu.SemaphoreType.DMA((4,)),
            pltpu.SemaphoreType.DMA((4,)),
        ],
        compiler_params=pltpu.CompilerParams(
            collective_id=0, has_side_effects=True, vmem_limit_bytes=56 * 1024 * 1024
        ),
        name="chain",
    )(row, scale, keep, gate_w, up_w, down_w)


def weights_kernel(u_ref, sgi_ref, gd_ref, ud_ref, hid_ref, gate_out, up_out, down_out):
    block, hidden_cols = gate_out.shape
    cols = min(256, hidden_cols)
    rows = min(128, block)
    for h in range(0, hidden_cols, cols):
        gate_delta = gd_ref[:, h : h + cols]
        up_delta = ud_ref[:, h : h + cols]
        for r in range(0, block, rows):
            picked = u_ref[:, r : r + rows]
            gate_out[r : r + rows, h : h + cols] = lax.dot_general(
                picked, gate_delta, FIRST, preferred_element_type=F32
            ).astype(BF16)
            up_out[r : r + rows, h : h + cols] = lax.dot_general(
                picked, up_delta, FIRST, preferred_element_type=F32
            ).astype(BF16)
    wide = min(256, block)
    for d in range(0, block, wide):
        slot_in = sgi_ref[:, d : d + wide]
        for h in range(0, hidden_cols, rows):
            down_out[h : h + rows, d : d + wide] = lax.dot_general(
                hid_ref[:, h : h + rows], slot_in, FIRST, preferred_element_type=F32
            ).astype(BF16)


def weight_gradients(u, sgi, gd, ud, hid):
    tokens, width = u.shape
    hidden_cols = gd.shape[1]
    block = 512 if width % 512 == 0 else width
    wide = pl.BlockSpec((tokens, block), lambda i: (0, i))
    whole = pl.BlockSpec((tokens, hidden_cols), lambda i: (0, 0))
    tall = pl.BlockSpec((block, hidden_cols), lambda i: (i, 0))
    shape = jax.ShapeDtypeStruct
    return pl.pallas_call(
        weights_kernel,
        grid=(width // block,),
        out_shape=(
            shape((width, hidden_cols), BF16),
            shape((width, hidden_cols), BF16),
            shape((hidden_cols, width), BF16),
        ),
        in_specs=[wide, wide, whole, whole, whole],
        out_specs=(tall, tall, pl.BlockSpec((hidden_cols, block), lambda i: (0, i))),
        compiler_params=pltpu.CompilerParams(vmem_limit_bytes=40 * 1024 * 1024),
        name="weight_gradients",
    )(u, sgi, gd, ud, hid)


def per_device(
    inputs,
    cotangent,
    gate_weight,
    up_weight,
    down_weight,
    route_rows,
    route_count,
    route_weight,
    width_mask,
):
    width = inputs.shape[2]
    n = lax.axis_size("et")
    seg = lax.axis_index("segment")
    slots = route_rows.shape[2]
    hidden_cols = gate_weight.shape[2]
    keep = jnp.repeat(width_mask.astype(F32), hidden_cols // width_mask.shape[1], axis=1)
    positions = jnp.arange(slots, dtype=jnp.int32)
    live = jnp.where(positions < route_count[0, 0], route_weight[0, 0], 0.0)
    hit = route_rows[0, 0][None, :] == positions[:, None]
    scale = jnp.sum(jnp.where(hit, live[None, :], 0.0), axis=1)
    scale = jnp.broadcast_to(scale[:, None], (slots, 128))
    row = jnp.where(seg == 0, inputs[0], cotangent[0]).reshape(FOLD, width // FOLD)
    first, second, u, sgi, gd, ud, hid = chain(
        n, row, scale, keep, gate_weight[0], up_weight[0], down_weight[0]
    )
    grad_gate, grad_up, grad_down = weight_gradients(u, sgi, gd, ud, hid)
    section = jnp.where(seg == 0, first, second).reshape(1, 1, 1, width)
    grad_in = jnp.where(seg == 0, second, first).reshape(1, 1, 1, width)
    return section, grad_in, grad_gate[None], grad_up[None], grad_down[None]


def solution(mesh):
    return jax.shard_map(
        per_device,
        mesh=mesh,
        in_specs=(
            P(None, "et", None),
            P(None, "et", None),
            P("segment", None, "et"),
            P("segment", None, "et"),
            P("segment", "et", None),
            P("segment", None, None),
            P("segment", None),
            P("segment", None, None),
            P("segment", "et"),
        ),
        out_specs=(
            P("segment", None, "et", None),
            P("segment", None, "et", None),
            P("segment", None, "et"),
            P("segment", None, "et"),
            P("segment", "et", None),
        ),
        check_vma=False,
    )
```

```python
import functools
import jax
import jax.numpy as jnp
from jax import lax
from jax.experimental import pallas as pl
from jax.experimental.pallas import tpu as pltpu
from jax.sharding import PartitionSpec as P

MESH = pl.DeviceIdType.MESH
F32 = jnp.float32
BF16 = jnp.bfloat16
FOLD = 16
LAST = (((1,), (1,)), ((), ()))
FIRST = (((0,), (0,)), ((), ()))


def chunk_of(width):
    for size in (1536, 768, 512, 256, 128):
        if width % size == 0:
            return size
    return width


def chain_kernel(
    n,
    chunk,
    row_ref,
    rows_ref,
    count_ref,
    weight_ref,
    mask_ref,
    gate_hbm,
    up_hbm,
    down_hbm,
    first_out,
    second_out,
    pack_ref,
    gate_w,
    up_w,
    down_w,
    first_all,
    second_all,
    send_a,
    send_b,
    recv_a,
    recv_b,
    fold_ref,
    part_ref,
    gate_val,
    up_val,
    scale_ref,
    keep_ref,
    load_sem,
    send_sem,
    recv_sem,
):
    seg = lax.axis_index("segment")
    me = lax.axis_index("et")
    other = 1 - seg
    width, hidden_cols = gate_w.shape
    tokens = pack_ref.shape[0]
    u_ref = pack_ref.at[:, pl.ds(0, width)]
    sgi_ref = pack_ref.at[:, pl.ds(width, width)]
    gd_ref = pack_ref.at[:, pl.ds(2 * width, hidden_cols)]
    ud_ref = pack_ref.at[:, pl.ds(2 * width + hidden_cols, hidden_cols)]
    hid_ref = pack_ref.at[:, pl.ds(2 * width + 2 * hidden_cols, hidden_cols)]
    quota = width // FOLD
    steps = width // chunk

    def span(c):
        return pl.ds(pl.multiple_of(c * chunk, chunk), chunk)

    def load_gate(c):
        return pltpu.make_async_copy(gate_hbm.at[span(c)], gate_w.at[span(c)], load_sem.at[0, c])

    def load_up(c):
        return pltpu.make_async_copy(up_hbm.at[span(c)], up_w.at[span(c)], load_sem.at[1, c])

    def load_down(c):
        return pltpu.make_async_copy(
            down_hbm.at[:, span(c)], down_w.at[:, span(c)], load_sem.at[2, c]
        )

    @pl.when(seg == 0)
    def _():
        for c in range(steps):
            load_gate(c).start()
            load_up(c).start()
        for c in range(steps):
            load_down(c).start()

    @pl.when(seg == 1)
    def _():
        for c in range(steps):
            load_down(c).start()
        for c in range(steps):
            load_gate(c).start()
            load_up(c).start()

    barrier = pltpu.get_barrier_semaphore()

    def greet(k, _):
        pl.semaphore_signal(barrier, inc=1, device_id=(other, k), device_id_type=MESH)
        return 0

    def greet_own(k, _):
        pl.semaphore_signal(
            barrier, inc=1, device_id=(seg, lax.rem(me + k, n)), device_id_type=MESH
        )
        return 0

    lax.fori_loop(1, n, greet_own, 0)
    lax.fori_loop(0, n, greet, 0)
    pl.semaphore_wait(barrier, 2 * n - 1)

    def remote(src, dst, stage, to_seg, to_et):
        return pltpu.make_async_remote_copy(
            src_ref=src,
            dst_ref=dst,
            send_sem=send_sem.at[stage],
            recv_sem=recv_sem.at[stage],
            device_id=(to_seg, to_et),
            device_id_type=MESH,
        )

    def wait_bytes(buffer, count, sem):
        piece = buffer.at[pl.ds(0, count)]
        pltpu.make_async_copy(piece, piece, sem).wait()

    def send_first():
        def body(k, _):
            remote(row_ref, first_all.at[me], 0, seg, lax.rem(me + k, n)).start()
            return 0

        lax.fori_loop(1, n, body, 0)
        first_all[pl.ds(me, 1)] = row_ref[...][None]

    def send_second(src):
        def body(k, _):
            remote(src, second_all.at[me], 1, other, lax.rem(me + k, n)).start()
            return 0

        lax.fori_loop(0, n, body, 0)

    def unfold(buffer, out, scaled):
        fold_ref[...] = buffer[...].astype(F32)
        for j in range(FOLD):
            piece = fold_ref[:, j, :]
            if scaled:
                piece = piece * scale_ref[:, 0:1]
            out[:, j * quota : (j + 1) * quota] = piece.astype(BF16)

    def scatter(send, recv, stage):
        for j in range(FOLD):
            fold_ref[:, j, :] = part_ref[:, j * quota : (j + 1) * quota]
        send[...] = fold_ref[...].astype(BF16)

        def body(k, _):
            peer = lax.rem(me + k, n)
            remote(send.at[peer], recv.at[me], stage, seg, peer).start()
            return 0

        lax.fori_loop(1, n, body, 0)
        recv[pl.ds(me, 1)] = send[pl.ds(me, 1)]

    def gathered_sum(recv, stage):
        wait_bytes(recv, n - 1, recv_sem.at[stage])

        def body(k, total):
            return total + recv[k].astype(F32)

        return lax.fori_loop(0, n, body, jnp.zeros((FOLD, quota), F32))

    def project():
        def body(c, carry):
            gate_acc, up_acc = carry
            load_gate(c).wait()
            load_up(c).wait()
            rows = u_ref[:, span(c)]
            gate_acc = gate_acc + jnp.dot(rows, gate_w[span(c), :], preferred_element_type=F32)
            up_acc = up_acc + jnp.dot(rows, up_w[span(c), :], preferred_element_type=F32)
            return gate_acc, up_acc

        zero = jnp.zeros((tokens, hidden_cols), F32)
        gate_acc, up_acc = lax.fori_loop(0, steps, body, (zero, zero))
        gate_val[...] = gate_acc
        up_val[...] = up_acc
        hid_ref[...] = (gate_acc * jax.nn.sigmoid(gate_acc) * up_acc * keep_ref[...]).astype(BF16)

    def outcome(loads):
        def body(c, _):
            if loads:
                load_down(c).wait()
            value = jnp.dot(hid_ref[...], down_w[:, span(c)], preferred_element_type=F32)
            part_ref[:, span(c)] = value * scale_ref[:, 0:1]
            return 0

        lax.fori_loop(0, steps, body, 0)

    def hidden_delta(loads):
        def body(c, acc):
            if loads:
                load_down(c).wait()
            return acc + lax.dot_general(
                sgi_ref[:, span(c)], down_w[:, span(c)], LAST, preferred_element_type=F32
            )

        return lax.fori_loop(0, steps, body, jnp.zeros((tokens, hidden_cols), F32))

    def deltas(delta):
        gate_value = gate_val[...]
        sig = jax.nn.sigmoid(gate_value)
        kept = delta * keep_ref[...]
        gd_ref[...] = (kept * up_val[...] * sig * (1.0 + gate_value * (1.0 - sig))).astype(BF16)
        ud_ref[...] = (kept * gate_value * sig).astype(BF16)

    def slot_gradient():
        def body(c, _):
            value = lax.dot_general(
                gd_ref[...], gate_w[span(c), :], LAST, preferred_element_type=F32
            )
            part_ref[:, span(c)] = value + lax.dot_general(
                ud_ref[...], up_w[span(c), :], LAST, preferred_element_type=F32
            )
            return 0

        lax.fori_loop(0, steps, body, 0)

    send_first()

    slots = rows_ref.shape[1]
    position = lax.broadcasted_iota(jnp.int32, (1, slots), 1)
    live = jnp.where(position < count_ref[...], weight_ref[...], 0.0)
    token = lax.broadcasted_iota(jnp.int32, (tokens, slots), 0)
    hit = jnp.where(rows_ref[...] == token, live, 0.0)
    scale_ref[...] = jnp.broadcast_to(jnp.sum(hit, axis=1, keepdims=True), scale_ref.shape)
    tiles = mask_ref.shape[1]
    tile = hidden_cols // tiles
    for t in range(tiles):
        kept = mask_ref[:, t : t + 1].astype(F32)
        keep_ref[:, t * tile : (t + 1) * tile] = jnp.broadcast_to(kept, (1, tile))

    @pl.when(seg == 0)
    def _():
        wait_bytes(first_all, n - 1, recv_sem.at[0])
        unfold(first_all, u_ref, False)
        project()
        outcome(True)
        scatter(send_a, recv_a, 2)
        total = gathered_sum(recv_a, 2)
        first_out[...] = (row_ref[...].astype(F32) + total).astype(BF16)
        send_second(first_out)
        wait_bytes(second_all, n, recv_sem.at[1])
        unfold(second_all, sgi_ref, True)
        deltas(hidden_delta(False))
        slot_gradient()
        scatter(send_b, recv_b, 3)
        total = gathered_sum(recv_b, 3)
        second_out[...] = (second_all[me].astype(F32) + total).astype(BF16)

    @pl.when(seg == 1)
    def _():
        wait_bytes(first_all, n - 1, recv_sem.at[0])
        unfold(first_all, sgi_ref, True)
        part_ref[:, 0:hidden_cols] = hidden_delta(True)
        wait_bytes(second_all, n, recv_sem.at[1])
        unfold(second_all, u_ref, False)
        project()
        deltas(part_ref[:, 0:hidden_cols])
        slot_gradient()
        scatter(send_a, recv_a, 2)
        total = gathered_sum(recv_a, 2)
        first_out[...] = (row_ref[...].astype(F32) + total).astype(BF16)
        send_second(first_out)
        outcome(False)
        scatter(send_b, recv_b, 3)
        total = gathered_sum(recv_b, 3)
        second_out[...] = (second_all[me].astype(F32) + total).astype(BF16)

    wait_bytes(first_all, n - 1, send_sem.at[0])
    wait_bytes(second_all, n, send_sem.at[1])
    wait_bytes(send_a, n - 1, send_sem.at[2])
    wait_bytes(send_b, n - 1, send_sem.at[3])


def chain(n, row, rows, count, weight, mask, gate_w, up_w, down_w):
    tokens = n
    width, hidden_cols = gate_w.shape
    quota = width // FOLD
    chunk = chunk_of(width)
    vmem = pl.BlockSpec(memory_space=pltpu.VMEM)
    hbm = pl.BlockSpec(memory_space=pl.ANY)
    shape = jax.ShapeDtypeStruct
    buffers = [pltpu.VMEM((n, FOLD, quota), BF16)] * 6
    return pl.pallas_call(
        functools.partial(chain_kernel, n, chunk),
        out_shape=(
            shape((FOLD, quota), BF16),
            shape((FOLD, quota), BF16),
            shape((tokens, 2 * width + 3 * hidden_cols), BF16),
        ),
        in_specs=[vmem] * 5 + [hbm] * 3,
        out_specs=(vmem,) * 3,
        scratch_shapes=[
            pltpu.VMEM((width, hidden_cols), BF16),
            pltpu.VMEM((width, hidden_cols), BF16),
            pltpu.VMEM((hidden_cols, width), BF16),
            *buffers,
            pltpu.VMEM((n, FOLD, quota), F32),
            pltpu.VMEM((tokens, width), F32),
            pltpu.VMEM((tokens, hidden_cols), F32),
            pltpu.VMEM((tokens, hidden_cols), F32),
            pltpu.VMEM((tokens, 128), F32),
            pltpu.VMEM((1, hidden_cols), F32),
            pltpu.SemaphoreType.DMA((3, width // chunk)),
            pltpu.SemaphoreType.DMA((4,)),
            pltpu.SemaphoreType.DMA((4,)),
        ],
        compiler_params=pltpu.CompilerParams(
            collective_id=0, has_side_effects=True, vmem_limit_bytes=56 * 1024 * 1024
        ),
        name="chain",
    )(row, rows, count, weight, mask, gate_w, up_w, down_w)


def weights_kernel(u_ref, sgi_ref, gd_ref, ud_ref, hid_ref, gate_out, up_out, down_out):
    block, hidden_cols = gate_out.shape
    cols = min(256, hidden_cols)
    rows = min(128, block)
    for h in range(0, hidden_cols, cols):
        gate_delta = gd_ref[:, h : h + cols]
        up_delta = ud_ref[:, h : h + cols]
        for r in range(0, block, rows):
            picked = u_ref[:, r : r + rows]
            gate_out[r : r + rows, h : h + cols] = lax.dot_general(
                picked, gate_delta, FIRST, preferred_element_type=F32
            ).astype(BF16)
            up_out[r : r + rows, h : h + cols] = lax.dot_general(
                picked, up_delta, FIRST, preferred_element_type=F32
            ).astype(BF16)
    wide = min(256, block)
    for d in range(0, block, wide):
        slot_in = sgi_ref[:, d : d + wide]
        for h in range(0, hidden_cols, rows):
            down_out[h : h + rows, d : d + wide] = lax.dot_general(
                hid_ref[:, h : h + rows], slot_in, FIRST, preferred_element_type=F32
            ).astype(BF16)


def weight_gradients(pack, width, hidden_cols):
    tokens = pack.shape[0]
    block = 512 if width % 512 == 0 else width
    blocks = width // block
    ahead = 2 * width // hidden_cols
    specs = [
        pl.BlockSpec((tokens, block), lambda i: (0, i)),
        pl.BlockSpec((tokens, block), lambda i: (0, blocks + i)),
        pl.BlockSpec((tokens, hidden_cols), lambda i: (0, ahead)),
        pl.BlockSpec((tokens, hidden_cols), lambda i: (0, ahead + 1)),
        pl.BlockSpec((tokens, hidden_cols), lambda i: (0, ahead + 2)),
    ]
    tall = pl.BlockSpec((block, hidden_cols), lambda i: (i, 0))
    shape = jax.ShapeDtypeStruct
    return pl.pallas_call(
        weights_kernel,
        grid=(width // block,),
        out_shape=(
            shape((width, hidden_cols), BF16),
            shape((width, hidden_cols), BF16),
            shape((hidden_cols, width), BF16),
        ),
        in_specs=specs,
        out_specs=(tall, tall, pl.BlockSpec((hidden_cols, block), lambda i: (0, i))),
        compiler_params=pltpu.CompilerParams(vmem_limit_bytes=40 * 1024 * 1024),
        name="weight_gradients",
    )(pack, pack, pack, pack, pack)


def per_device(
    inputs,
    cotangent,
    gate_weight,
    up_weight,
    down_weight,
    route_rows,
    route_count,
    route_weight,
    width_mask,
):
    width = inputs.shape[2]
    n = lax.axis_size("et")
    seg = lax.axis_index("segment")
    hidden_cols = gate_weight.shape[2]
    row = jnp.where(seg == 0, inputs[0], cotangent[0]).reshape(FOLD, width // FOLD)
    first, second, pack = chain(
        n,
        row,
        route_rows[0],
        route_count,
        route_weight[0],
        width_mask,
        gate_weight[0],
        up_weight[0],
        down_weight[0],
    )
    grad_gate, grad_up, grad_down = weight_gradients(pack, width, hidden_cols)
    section = jnp.where(seg == 0, first, second).reshape(1, 1, 1, width)
    grad_in = jnp.where(seg == 0, second, first).reshape(1, 1, 1, width)
    return section, grad_in, grad_gate[None], grad_up[None], grad_down[None]


def solution(mesh):
    return jax.shard_map(
        per_device,
        mesh=mesh,
        in_specs=(
            P(None, "et", None),
            P(None, "et", None),
            P("segment", None, "et"),
            P("segment", None, "et"),
            P("segment", "et", None),
            P("segment", None, None),
            P("segment", None),
            P("segment", None, None),
            P("segment", "et"),
        ),
        out_specs=(
            P("segment", None, "et", None),
            P("segment", None, "et", None),
            P("segment", None, "et"),
            P("segment", None, "et"),
            P("segment", "et", None),
        ),
        check_vma=False,
    )
```

```python
import functools
import jax
import jax.numpy as jnp
from jax import lax
from jax.experimental import pallas as pl
from jax.experimental.pallas import tpu as pltpu
from jax.sharding import PartitionSpec as P

MESH = pl.DeviceIdType.MESH
F32 = jnp.float32
BF16 = jnp.bfloat16
FOLD = 16
LAST = (((1,), (1,)), ((), ()))


def chunk_of(width):
    for size in (1536, 768, 512, 256, 128):
        if width % size == 0:
            return size
    return width


def chain_kernel(
    n,
    chunk,
    row_ref,
    rows_ref,
    count_ref,
    weight_ref,
    mask_ref,
    gate_hbm,
    up_hbm,
    down_hbm,
    section_out,
    grad_out,
    pack_ref,
    gate_w,
    up_w,
    down_w,
    first_all,
    second_all,
    send_a,
    send_b,
    recv_a,
    recv_b,
    fold_ref,
    part_ref,
    gate_val,
    up_val,
    scale_ref,
    keep_ref,
    load_sem,
    send_sem,
    recv_sem,
):
    seg = lax.axis_index("segment")
    me = lax.axis_index("et")
    other = 1 - seg
    width, hidden_cols = gate_w.shape
    tokens = pack_ref.shape[0]
    u_ref = pack_ref.at[:, pl.ds(0, width)]
    sgi_ref = pack_ref.at[:, pl.ds(width, width)]
    gd_ref = pack_ref.at[:, pl.ds(2 * width, hidden_cols)]
    ud_ref = pack_ref.at[:, pl.ds(2 * width + hidden_cols, hidden_cols)]
    hid_ref = pack_ref.at[:, pl.ds(2 * width + 2 * hidden_cols, hidden_cols)]
    quota = width // FOLD
    steps = width // chunk

    def span(c):
        return pl.ds(pl.multiple_of(c * chunk, chunk), chunk)

    big = 2 * chunk if steps % 2 == 0 else chunk

    def big_span(c):
        return pl.ds(pl.multiple_of(c * big, big), big)

    def load_gate(c):
        return pltpu.make_async_copy(gate_hbm.at[span(c)], gate_w.at[span(c)], load_sem.at[0, c])

    def load_up(c):
        return pltpu.make_async_copy(up_hbm.at[span(c)], up_w.at[span(c)], load_sem.at[1, c])

    def load_down(c):
        return pltpu.make_async_copy(
            down_hbm.at[:, span(c)], down_w.at[:, span(c)], load_sem.at[2, c]
        )

    @pl.when(seg == 0)
    def _():
        for c in range(steps):
            load_gate(c).start()
            load_up(c).start()
        for c in range(steps):
            load_down(c).start()

    @pl.when(seg == 1)
    def _():
        for c in range(steps):
            load_down(c).start()
        for c in range(steps):
            load_gate(c).start()
            load_up(c).start()

    barrier = pltpu.get_barrier_semaphore()

    def greet(k, _):
        pl.semaphore_signal(barrier, inc=1, device_id=(other, k), device_id_type=MESH)
        return 0

    def greet_own(k, _):
        pl.semaphore_signal(
            barrier, inc=1, device_id=(seg, lax.rem(me + k, n)), device_id_type=MESH
        )
        return 0

    lax.fori_loop(1, n, greet_own, 0)
    lax.fori_loop(0, n, greet, 0)
    pl.semaphore_wait(barrier, 2 * n - 1)

    def remote(src, dst, stage, to_seg, to_et):
        return pltpu.make_async_remote_copy(
            src_ref=src,
            dst_ref=dst,
            send_sem=send_sem.at[stage],
            recv_sem=recv_sem.at[stage],
            device_id=(to_seg, to_et),
            device_id_type=MESH,
        )

    def wait_bytes(buffer, count, sem):
        piece = buffer.at[pl.ds(0, count)]
        pltpu.make_async_copy(piece, piece, sem).wait()

    def send_first():
        def body(k, _):
            remote(row_ref, first_all.at[me], 0, seg, lax.rem(me + k, n)).start()
            return 0

        lax.fori_loop(1, n, body, 0)
        first_all[pl.ds(me, 1)] = row_ref[...][None]

    def send_second(src):
        def body(k, _):
            remote(src, second_all.at[me], 1, other, lax.rem(me + k, n)).start()
            return 0

        lax.fori_loop(0, n, body, 0)

    def unfold(buffer, out, scaled):
        fold_ref[...] = buffer[...].astype(F32)
        for j in range(FOLD):
            piece = fold_ref[:, j, :]
            if scaled:
                piece = piece * scale_ref[:, 0:1]
            out[:, j * quota : (j + 1) * quota] = piece.astype(BF16)

    def scatter(send, recv, stage):
        for j in range(FOLD):
            fold_ref[:, j, :] = part_ref[:, j * quota : (j + 1) * quota]
        send[...] = fold_ref[...].astype(BF16)

        def body(k, _):
            peer = lax.rem(me + k, n)
            remote(send.at[peer], recv.at[me], stage, seg, peer).start()
            return 0

        lax.fori_loop(1, n, body, 0)
        recv[pl.ds(me, 1)] = send[pl.ds(me, 1)]

    def gathered_sum(recv, stage):
        wait_bytes(recv, n - 1, recv_sem.at[stage])

        def body(k, total):
            return total + recv[k].astype(F32)

        return lax.fori_loop(0, n, body, jnp.zeros((FOLD, quota), F32))

    def project():
        def body(c, carry):
            gate_acc, up_acc = carry
            load_gate(c).wait()
            load_up(c).wait()
            rows = u_ref[:, span(c)]
            gate_acc = gate_acc + jnp.dot(rows, gate_w[span(c), :], preferred_element_type=F32)
            up_acc = up_acc + jnp.dot(rows, up_w[span(c), :], preferred_element_type=F32)
            return gate_acc, up_acc

        zero = jnp.zeros((tokens, hidden_cols), F32)
        gate_acc, up_acc = lax.fori_loop(0, steps, body, (zero, zero))
        gate_val[...] = gate_acc
        up_val[...] = up_acc
        hid_ref[...] = (gate_acc * jax.nn.sigmoid(gate_acc) * up_acc * keep_ref[...]).astype(BF16)

    def outcome(loads):
        def body(c, _):
            if loads:
                load_down(c).wait()
            value = jnp.dot(hid_ref[...], down_w[:, span(c)], preferred_element_type=F32)
            part_ref[:, span(c)] = value * scale_ref[:, 0:1]
            return 0

        lax.fori_loop(0, steps, body, 0)

    def hidden_delta(loads):
        def body(c, acc):
            part = span(c) if loads else big_span(c)
            if loads:
                load_down(c).wait()
            return acc + lax.dot_general(
                sgi_ref[:, part], down_w[:, part], LAST, preferred_element_type=F32
            )

        count = steps if loads else width // big
        return lax.fori_loop(0, count, body, jnp.zeros((tokens, hidden_cols), F32))

    def deltas(delta):
        gate_value = gate_val[...]
        sig = jax.nn.sigmoid(gate_value)
        kept = delta * keep_ref[...]
        gd_ref[...] = (kept * up_val[...] * sig * (1.0 + gate_value * (1.0 - sig))).astype(BF16)
        ud_ref[...] = (kept * gate_value * sig).astype(BF16)

    def slot_gradient():
        def body(c, _):
            value = lax.dot_general(
                gd_ref[...], gate_w[big_span(c), :], LAST, preferred_element_type=F32
            )
            part_ref[:, big_span(c)] = value + lax.dot_general(
                ud_ref[...], up_w[big_span(c), :], LAST, preferred_element_type=F32
            )
            return 0

        lax.fori_loop(0, width // big, body, 0)

    send_first()

    slots = rows_ref.shape[1]
    position = lax.broadcasted_iota(jnp.int32, (1, slots), 1)
    live = jnp.where(position < count_ref[...], weight_ref[...], 0.0)
    token = lax.broadcasted_iota(jnp.int32, (tokens, slots), 0)
    hit = jnp.where(rows_ref[...] == token, live, 0.0)
    scale_ref[...] = jnp.broadcast_to(jnp.sum(hit, axis=1, keepdims=True), scale_ref.shape)
    tiles = mask_ref.shape[1]
    tile = hidden_cols // tiles
    for t in range(tiles):
        kept = mask_ref[:, t : t + 1].astype(F32)
        keep_ref[:, t * tile : (t + 1) * tile] = jnp.broadcast_to(kept, (1, tile))

    @pl.when(seg == 0)
    def _():
        wait_bytes(first_all, n - 1, recv_sem.at[0])
        unfold(first_all, u_ref, False)
        project()
        outcome(True)
        scatter(send_a, recv_a, 2)
        total = gathered_sum(recv_a, 2)
        section_out[...] = (row_ref[...].astype(F32) + total).astype(BF16)
        send_second(section_out)
        wait_bytes(second_all, n, recv_sem.at[1])
        unfold(second_all, sgi_ref, True)
        deltas(hidden_delta(False))
        slot_gradient()
        scatter(send_b, recv_b, 3)
        total = gathered_sum(recv_b, 3)
        grad_out[...] = (second_all[me].astype(F32) + total).astype(BF16)

    @pl.when(seg == 1)
    def _():
        wait_bytes(first_all, n - 1, recv_sem.at[0])
        unfold(first_all, sgi_ref, True)
        part_ref[:, 0:hidden_cols] = hidden_delta(True)
        wait_bytes(second_all, n, recv_sem.at[1])
        unfold(second_all, u_ref, False)
        project()
        deltas(part_ref[:, 0:hidden_cols])
        slot_gradient()
        scatter(send_a, recv_a, 2)
        total = gathered_sum(recv_a, 2)
        grad_out[...] = (row_ref[...].astype(F32) + total).astype(BF16)
        send_second(grad_out)
        outcome(False)
        scatter(send_b, recv_b, 3)
        total = gathered_sum(recv_b, 3)
        section_out[...] = (second_all[me].astype(F32) + total).astype(BF16)

    wait_bytes(first_all, n - 1, send_sem.at[0])
    wait_bytes(second_all, n, send_sem.at[1])
    wait_bytes(send_a, n - 1, send_sem.at[2])
    wait_bytes(send_b, n - 1, send_sem.at[3])


def chain(n, row, rows, count, weight, mask, gate_w, up_w, down_w):
    tokens = n
    width, hidden_cols = gate_w.shape
    quota = width // FOLD
    chunk = chunk_of(width)
    vmem = pl.BlockSpec(memory_space=pltpu.VMEM)
    hbm = pl.BlockSpec(memory_space=pl.ANY)
    shape = jax.ShapeDtypeStruct
    buffers = [pltpu.VMEM((n, FOLD, quota), BF16)] * 6
    return pl.pallas_call(
        functools.partial(chain_kernel, n, chunk),
        out_shape=(
            shape((FOLD, quota), BF16),
            shape((FOLD, quota), BF16),
            shape((tokens, 2 * width + 3 * hidden_cols), BF16),
        ),
        in_specs=[vmem] * 5 + [hbm] * 3,
        out_specs=(vmem,) * 3,
        scratch_shapes=[
            pltpu.VMEM((width, hidden_cols), BF16),
            pltpu.VMEM((width, hidden_cols), BF16),
            pltpu.VMEM((hidden_cols, width), BF16),
            *buffers,
            pltpu.VMEM((n, FOLD, quota), F32),
            pltpu.VMEM((tokens, width), F32),
            pltpu.VMEM((tokens, hidden_cols), F32),
            pltpu.VMEM((tokens, hidden_cols), F32),
            pltpu.VMEM((tokens, 128), F32),
            pltpu.VMEM((1, hidden_cols), F32),
            pltpu.SemaphoreType.DMA((3, width // chunk)),
            pltpu.SemaphoreType.DMA((4,)),
            pltpu.SemaphoreType.DMA((4,)),
        ],
        compiler_params=pltpu.CompilerParams(
            collective_id=0, has_side_effects=True, vmem_limit_bytes=56 * 1024 * 1024
        ),
        name="chain",
    )(row, rows, count, weight, mask, gate_w, up_w, down_w)


def turned(value):
    return jnp.transpose(value.astype(F32)).astype(BF16)


def weights_kernel(
    u_ref, sgi_ref, gd_ref, ud_ref, hid_ref, gate_out, up_out, down_out, u_turned, hid_turned
):
    block, hidden_cols = gate_out.shape
    cols = min(256, hidden_cols)
    rows = min(128, block)

    @pl.when(pl.program_id(0) == 0)
    def _():
        hid_turned[...] = turned(hid_ref[...])

    u_turned[...] = turned(u_ref[...])
    for h in range(0, hidden_cols, cols):
        gate_delta = gd_ref[:, h : h + cols]
        up_delta = ud_ref[:, h : h + cols]
        for r in range(0, block, rows):
            picked = u_turned[r : r + rows, :]
            gate_out[r : r + rows, h : h + cols] = jnp.dot(
                picked, gate_delta, preferred_element_type=F32
            ).astype(BF16)
            up_out[r : r + rows, h : h + cols] = jnp.dot(
                picked, up_delta, preferred_element_type=F32
            ).astype(BF16)
    wide = min(256, block)
    for d in range(0, block, wide):
        slot_in = sgi_ref[:, d : d + wide]
        for h in range(0, hidden_cols, rows):
            down_out[h : h + rows, d : d + wide] = jnp.dot(
                hid_turned[h : h + rows, :], slot_in, preferred_element_type=F32
            ).astype(BF16)


def weight_gradients(pack, width, hidden_cols):
    tokens = pack.shape[0]
    block = 512 if width % 512 == 0 else width
    blocks = width // block
    ahead = 2 * width // hidden_cols
    specs = [
        pl.BlockSpec((tokens, block), lambda i: (0, i)),
        pl.BlockSpec((tokens, block), lambda i: (0, blocks + i)),
        pl.BlockSpec((tokens, hidden_cols), lambda i: (0, ahead)),
        pl.BlockSpec((tokens, hidden_cols), lambda i: (0, ahead + 1)),
        pl.BlockSpec((tokens, hidden_cols), lambda i: (0, ahead + 2)),
    ]
    tall = pl.BlockSpec((block, hidden_cols), lambda i: (i, 0))
    shape = jax.ShapeDtypeStruct
    return pl.pallas_call(
        weights_kernel,
        grid=(width // block,),
        out_shape=(
            shape((width, hidden_cols), BF16),
            shape((width, hidden_cols), BF16),
            shape((hidden_cols, width), BF16),
        ),
        in_specs=specs,
        out_specs=(tall, tall, pl.BlockSpec((hidden_cols, block), lambda i: (0, i))),
        scratch_shapes=[
            pltpu.VMEM((block, tokens), BF16),
            pltpu.VMEM((hidden_cols, tokens), BF16),
        ],
        compiler_params=pltpu.CompilerParams(vmem_limit_bytes=40 * 1024 * 1024),
        name="weight_gradients",
    )(pack, pack, pack, pack, pack)


def per_device(
    inputs,
    cotangent,
    gate_weight,
    up_weight,
    down_weight,
    route_rows,
    route_count,
    route_weight,
    width_mask,
):
    width = inputs.shape[2]
    n = lax.axis_size("et")
    seg = lax.axis_index("segment")
    hidden_cols = gate_weight.shape[2]
    row = jnp.where(seg == 0, inputs[0], cotangent[0]).reshape(FOLD, width // FOLD)
    section, grad_in, pack = chain(
        n,
        row,
        route_rows[0],
        route_count,
        route_weight[0],
        width_mask,
        gate_weight[0],
        up_weight[0],
        down_weight[0],
    )
    grad_gate, grad_up, grad_down = weight_gradients(pack, width, hidden_cols)
    section = section.reshape(1, 1, 1, width)
    grad_in = grad_in.reshape(1, 1, 1, width)
    return section, grad_in, grad_gate[None], grad_up[None], grad_down[None]


def solution(mesh):
    return jax.shard_map(
        per_device,
        mesh=mesh,
        in_specs=(
            P(None, "et", None),
            P(None, "et", None),
            P("segment", None, "et"),
            P("segment", None, "et"),
            P("segment", "et", None),
            P("segment", None, None),
            P("segment", None),
            P("segment", None, None),
            P("segment", "et"),
        ),
        out_specs=(
            P("segment", None, "et", None),
            P("segment", None, "et", None),
            P("segment", None, "et"),
            P("segment", None, "et"),
            P("segment", "et", None),
        ),
        check_vma=False,
    )
```
